32 devices in a mesh: dp: 8 (over z, y), mp: 4 (over x, core).
Axes of the slice: x: 2, y: 2, z: 4, core: 2. Of those that a mesh axis runs over, the one named last changes fastest.
Arguments:
- tokens: bfloat16 [128, 8192], P('dp', 'mp'), may hold values from -6 to 6
- gate_weight: bfloat16 [8192, 21504], P('mp', 'dp'), may hold values from -0.0625 to 0.0625
- up_weight: bfloat16 [8192, 21504], P('mp', 'dp'), may hold values from -0.0625 to 0.0625
- down_weight: bfloat16 [21504, 8192], P('dp', 'mp'), may hold values from -0.0390625 to 0.0390625
Outputs:
- mixed_out: bfloat16 [128, 8192], P('dp', 'mp')
The draws below stay inside these ranges and needn't reach their ends.
All inputs are finite; a program needn't handle non-finite values.
Results may differ from the reference program's by a relative error of at most 0.005.
Values may be sent and summed in bfloat16 or wider, within the bound.
A program may use at most 128 MiB of HBM per device.

```python
import jax
import jax.numpy as jnp

D = 8192
FF = 21504
TOKENS = 128


def steps_of(key, extent, split, least, largest):
    def one(dim, parts):
        draws = jax.random.uniform(jax.random.fold_in(jax.random.fold_in(key, 6), dim), (parts,), jnp.float32, least / len(split), largest / len(split))
        return jnp.repeat(jnp.exp(draws), extent[dim] // parts).reshape((-1,) + (1,) * (len(extent) - dim - 1))

    loudness = one(*split[0])
    for cut in split[1:]:
        loudness = loudness * one(*cut)
    return loudness


def bell_draw(key, shape, spread, reach, pieces=(), dtype=jnp.bfloat16):
    drawn = spread * jax.random.normal(key, shape, jnp.float32)
    if pieces:
        drawn = drawn * steps_of(key, shape, pieces, -0.22, 0.18)
    return jnp.clip(drawn, -reach, reach).astype(dtype)


def setup_inputs(seed: int = 0) -> dict:
    streams_of = jax.random.split(jax.random.key(seed), 5)
    return {
        "tokens": bell_draw(streams_of[0], (TOKENS, D), 1.0, 6.0, ((0, 8), (1, 4))),
        "gate_weight": bell_draw(streams_of[1], (D, FF), D ** -0.5, 0.0625, ((0, 4), (1, 8))),
        "up_weight": bell_draw(streams_of[2], (D, FF), D ** -0.5, 0.0625, ((0, 4), (1, 8))),
        "down_weight": bell_draw(streams_of[3], (FF, D), FF ** -0.5, 0.0390625, ((0, 8), (1, 4))),
    }


def reference(tokens, gate_weight, up_weight, down_weight):
    gate_sum = jnp.dot(tokens, gate_weight, preferred_element_type=jnp.float32)
    up_sum = jnp.dot(tokens, up_weight, preferred_element_type=jnp.float32)
    hidden = (jax.nn.silu(gate_sum) * up_sum).astype(jnp.bfloat16)
    return jnp.dot(hidden, down_weight, preferred_element_type=jnp.float32).astype(jnp.bfloat16)
```

```python
import functools

import jax
import jax.numpy as jnp
from jax import lax
from jax.experimental import pallas as pl
from jax.experimental.pallas import tpu as pltpu
from jax.sharding import PartitionSpec as P

MESH = pl.DeviceIdType.MESH
F32, BF16 = jnp.float32, jnp.bfloat16


def cuts(extent, size):
    out, at = [], 0
    while at < extent:
        out.append((at, min(size, extent - at)))
        at += size
    return out


def tiles(extent):
    step = 256 if extent % 256 == 0 else extent
    return extent // step, step


class Copies:
    def __init__(self):
        self.sent = []

    def start(self, src, dst, send_sem, recv_sem, device):
        copy = pltpu.make_async_remote_copy(
            src_ref=src, dst_ref=dst, send_sem=send_sem, recv_sem=recv_sem,
            device_id=device, device_id_type=MESH,
        )
        copy.start()
        self.sent.append(copy)


def arrived(dst, send_sem, recv_sem, device):
    pltpu.make_async_remote_copy(
        src_ref=dst, dst_ref=dst, send_sem=send_sem, recv_sem=recv_sem,
        device_id=device, device_id_type=MESH,
    ).wait_recv()


def kernel(Z, R, ff_cuts, out_cuts, tok_hbm, gate_hbm, up_hbm, down_hbm, out_ref, s):
    dp, mp = lax.axis_index("dp"), lax.axis_index("mp")
    z, y = lax.div(dp, 2), lax.rem(dp, 2)
    x, core = lax.div(mp, 2), lax.rem(mp, 2)
    C = len(ff_cuts)

    def zdev(d):
        return (lax.rem(z + d, Z) * 2 + y, mp)

    def xdev(d):
        return (dp, lax.rem(x + d, R) * 2 + core)

    ydev = (z * 2 + 1 - y, mp)
    sib = (dp, x * 2 + 1 - core)

    own = pltpu.make_async_copy(tok_hbm, s["tok"].at[z, y], s["own_sem"])
    own.start()
    loads = []
    for c, (at, n) in enumerate(ff_cuts):
        pair = [
            pltpu.make_async_copy(w.at[:, pl.ds(at, n)], s["wgu"][c].at[g], s["w_sem"].at[g, c])
            for g, w in enumerate((gate_hbm, up_hbm))
        ]
        for p in pair:
            p.start()
        loads.append(pair)
    downs = []
    for c, (at, n) in enumerate(ff_cuts):
        p = pltpu.make_async_copy(down_hbm.at[pl.ds(at, n)], s["wd"][c], s["w_sem"].at[2, c])
        p.start()
        downs.append(p)

    barrier = pltpu.get_barrier_semaphore()
    peers = [ydev, sib] + [zdev(d) for d in range(1, Z)] + [xdev(d) for d in range(1, R)]
    for peer in peers:
        pl.semaphore_signal(barrier, inc=1, device_id=peer, device_id_type=MESH)
    pl.semaphore_wait(barrier, len(peers))

    copies = Copies()
    tok = s["tok"]

    for d in range(1, Z):
        copies.start(tok_hbm, tok.at[z, y], s["tz_sem"].at[0, d], s["tz_sem"].at[1, d], zdev(d))
    copies.start(tok_hbm, tok.at[z, y], s["ty_sem"].at[0, 0], s["ty_sem"].at[1, 0], ydev)
    for d in range(1, Z):
        block = tok.at[lax.rem(z + Z - d, Z), y]
        arrived(block, s["tz_sem"].at[0, d], s["tz_sem"].at[1, d], zdev(d))
        copies.start(block, block, s["ty_sem"].at[0, d], s["ty_sem"].at[1, d], ydev)
    for d in range(Z):
        block = tok.at[lax.rem(z + Z - d, Z), 1 - y]
        arrived(block, s["ty_sem"].at[0, d], s["ty_sem"].at[1, d], ydev)
    own.wait()

    rows = tok.shape[0] * 2 * tok.shape[2]
    width = tok.shape[3]
    q = rows // (2 * R)

    def project(c):
        n = ff_cuts[c][1]
        count, step = tiles(n)
        part, w = s["part"][c], s["wgu"][c]
        for g in range(2):
            loads[c][g].wait()

        def body(j, _):
            cols = pl.ds(pl.multiple_of(j * step, 128), step) if count > 1 else slice(None)
            for g in range(2):
                p = jnp.dot(
                    tok[...].reshape(rows, width), w[g, :, cols], preferred_element_type=F32
                ).reshape(R, 2, q, step)
                for k in range(2):
                    part[k, g, :, :, cols] = p[:, k]
            return 0

        if count > 1:
            lax.fori_loop(0, count, body, 0)
        else:
            body(0, 0)
        copies.start(
            part.at[1 - core], s["rx1"][c], s["s1_sem"].at[0, c], s["s1_sem"].at[1, c], sib
        )

    def share(c):
        part, rx1 = s["part"][c], s["rx1"][c]
        arrived(rx1, s["s1_sem"].at[0, c], s["s1_sem"].at[1, c], sib)
        for d in range(1, R):
            r = lax.rem(x + d, R)
            for g in range(2):
                s["tx2"][c][d - 1, g] = (part[core, g, r] + rx1[g, r]).astype(BF16)
            copies.start(
                s["tx2"][c].at[d - 1], s["rx2"][c].at[d - 1],
                s["s2_sem"].at[0, c, d], s["s2_sem"].at[1, c, d], xdev(d),
            )

    def activate(c):
        part, rx1, rx2, hid = s["part"][c], s["rx1"][c], s["rx2"][c], s["hid"][c]
        for d in range(1, R):
            arrived(rx2.at[d - 1], s["s2_sem"].at[0, c, d], s["s2_sem"].at[1, c, d], xdev(d))
        sums = []
        for g in range(2):
            v = part[core, g, x] + rx1[g, x]
            for d in range(1, R):
                v = v + rx2[d - 1, g].astype(F32)
            sums.append(v)
        gate, up = sums
        hid[x, core] = (gate / (1.0 + jnp.exp(-gate)) * up).astype(BF16)
        block = hid.at[x, core]
        for d in range(1, R):
            copies.start(
                block, block, s["s3_sem"].at[0, c, d], s["s3_sem"].at[1, c, d], xdev(d)
            )
        copies.start(block, block, s["s4_sem"].at[0, c, 0], s["s4_sem"].at[1, c, 0], sib)

    def forward(c):
        hid = s["hid"][c]
        for d in range(1, R):
            block = hid.at[lax.rem(x + R - d, R), core]
            arrived(block, s["s3_sem"].at[0, c, d], s["s3_sem"].at[1, c, d], xdev(d))
            copies.start(block, block, s["s4_sem"].at[0, c, d], s["s4_sem"].at[1, c, d], sib)

    acc = s["acc"]

    def mix(c, first, last):
        n = ff_cuts[c][1]
        hid, wd = s["hid"][c], s["wd"][c]
        for d in range(R):
            block = hid.at[lax.rem(x + R - d, R), 1 - core]
            arrived(block, s["s4_sem"].at[0, c, d], s["s4_sem"].at[1, c, d], sib)
        downs[c].wait()
        for j, (at, m) in enumerate(out_cuts):
            count, step = tiles(m)

            def body(i, _):
                cols = pl.ds(pl.multiple_of(at + i * step, 128), step)
                p = jnp.dot(
                    hid[...].reshape(rows, n), wd[:, cols], preferred_element_type=F32
                ).reshape(Z, 2, rows // (2 * Z), step)
                if not first:
                    p = p + acc[:, :, :, cols]
                acc[:, :, :, cols] = p
                return 0

            lax.fori_loop(0, count, body, 0)
            if last:
                ysend(j)

    def ysend(j):
        at, m = out_cuts[j]
        for k in range(Z):
            s["ty"][j][k] = acc[k, 1 - y, :, at:at + m].astype(BF16)
        copies.start(s["ty"][j], s["ry"][j], s["y_sem"].at[0, j], s["y_sem"].at[1, j], ydev)

    def zsend(j):
        at, m = out_cuts[j]
        ry = s["ry"][j]
        arrived(ry, s["y_sem"].at[0, j], s["y_sem"].at[1, j], ydev)
        for d in range(1, Z):
            k = lax.rem(z + d, Z)
            s["tz"][j][d - 1] = (acc[k, y, :, at:at + m] + ry[k].astype(F32)).astype(BF16)
            copies.start(
                s["tz"][j].at[d - 1], s["rz"][j].at[d - 1],
                s["z_sem"].at[0, j, d], s["z_sem"].at[1, j, d], zdev(d),
            )

    def finish(j):
        at, m = out_cuts[j]
        rz = s["rz"][j]
        v = acc[z, y, :, at:at + m] + s["ry"][j][z].astype(F32)
        for d in range(1, Z):
            arrived(rz.at[d - 1], s["z_sem"].at[0, j, d], s["z_sem"].at[1, j, d], zdev(d))
            v = v + rz[d - 1].astype(F32)
        out_ref[:, at:at + m] = v.astype(BF16)

    for c in range(C):
        project(c)
        if c:
            share(c - 1)
    if C > 1:
        activate(0)
    share(C - 1)
    for c in range(min(C, 1), C):
        activate(c)
        if c:
            forward(c - 1)
        if c > 1:
            mix(c - 2, c == 2, False)
    if C == 1:
        activate(0)
    forward(C - 1)
    if C > 1:
        mix(C - 2, C == 2, False)
    mix(C - 1, C == 1, True)
    for j in range(len(out_cuts)):
        zsend(j)
    for j in range(len(out_cuts)):
        finish(j)
    for copy in copies.sent:
        copy.wait_send()


def shards(ndp, nmp, tokens, gate_weight, up_weight, down_weight):
    Z, R = ndp // 2, nmp // 2
    t, width = tokens.shape
    hidden, features = down_weight.shape
    ff_cuts, out_cuts = cuts(hidden, 512), cuts(features, 512)
    C, J = len(ff_cuts), len(out_cuts)
    q = t * ndp // nmp
    dma = pltpu.SemaphoreType.DMA
    V = pltpu.VMEM
    scratch = {
        "tok": V((Z, 2, t, width), BF16),
        "wgu": [V((2, width, n), BF16) for _, n in ff_cuts],
        "wd": [V((n, features), BF16) for _, n in ff_cuts],
        "part": [V((2, 2, R, q, n), F32) for _, n in ff_cuts],
        "rx1": [V((2, R, q, n), F32) for _, n in ff_cuts],
        "tx2": [V((R - 1, 2, q, n), BF16) for _, n in ff_cuts],
        "rx2": [V((R - 1, 2, q, n), BF16) for _, n in ff_cuts],
        "hid": [V((R, 2, q, n), BF16) for _, n in ff_cuts],
        "acc": V((Z, 2, t, features), F32),
        "ty": [V((Z, t, m), BF16) for _, m in out_cuts],
        "ry": [V((Z, t, m), BF16) for _, m in out_cuts],
        "tz": [V((Z - 1, t, m), BF16) for _, m in out_cuts],
        "rz": [V((Z - 1, t, m), BF16) for _, m in out_cuts],
        "own_sem": dma,
        "w_sem": dma((3, C)),
        "tz_sem": dma((2, Z)),
        "ty_sem": dma((2, Z)),
        "s1_sem": dma((2, C)),
        "s2_sem": dma((2, C, R)),
        "s3_sem": dma((2, C, R)),
        "s4_sem": dma((2, C, R)),
        "y_sem": dma((2, J)),
        "z_sem": dma((2, J, Z)),
    }
    leaves, tree = jax.tree.flatten(scratch)

    def body(*refs):
        kernel(Z, R, ff_cuts, out_cuts, *refs[:5], jax.tree.unflatten(tree, refs[5:]))

    flops = 6 * t * ndp * width * hidden
    return pl.pallas_call(
        body,
        out_shape=jax.ShapeDtypeStruct((t, features), BF16),
        in_specs=[pl.BlockSpec(memory_space=pl.ANY)] * 4,
        out_specs=pl.BlockSpec(memory_space=pltpu.VMEM),
        scratch_shapes=leaves,
        compiler_params=pltpu.CompilerParams(
            collective_id=0, has_side_effects=True, vmem_limit_bytes=58 * 2**20
        ),
        cost_estimate=pl.CostEstimate(
            flops=flops, bytes_accessed=6 * width * hidden, transcendentals=0
        ),
        name="ffn",
    )(tokens, gate_weight, up_weight, down_weight)


def solution(mesh):
    return jax.shard_map(
        functools.partial(shards, mesh.shape["dp"], mesh.shape["mp"]),
        mesh=mesh,
        in_specs=(P("dp", "mp"), P("mp", "dp"), P("mp", "dp"), P("dp", "mp")),
        out_specs=P("dp", "mp"),
        check_vma=False,
    )
```

```python
import functools

import jax
import jax.numpy as jnp
from jax import lax
from jax.experimental import pallas as pl
from jax.experimental.pallas import tpu as pltpu
from jax.sharding import PartitionSpec as P

MESH = pl.DeviceIdType.MESH
F32, BF16 = jnp.float32, jnp.bfloat16


def cuts(extent, size):
    out, at = [], 0
    while at < extent:
        out.append((at, min(size, extent - at)))
        at += size
    return out


def tiles(extent):
    step = next((k for k in (768, 512, 384, 256) if extent % k == 0), extent)
    return extent // step, step


class Copies:
    def __init__(self):
        self.sent = []

    def make(self, src, dst, send_sem, recv_sem, device):
        copy = pltpu.make_async_remote_copy(
            src_ref=src, dst_ref=dst, send_sem=send_sem, recv_sem=recv_sem,
            device_id=device, device_id_type=MESH,
        )
        self.sent.append(copy)
        return copy

    def start(self, *args):
        self.make(*args).start()


def arrived(dst, send_sem, recv_sem, device):
    pltpu.make_async_remote_copy(
        src_ref=dst, dst_ref=dst, send_sem=send_sem, recv_sem=recv_sem,
        device_id=device, device_id_type=MESH,
    ).wait_recv()


def kernel(Z, R, ff_cuts, out_cuts, tok_hbm, gate_hbm, up_hbm, down_hbm, out_ref, s):
    dp, mp = lax.axis_index("dp"), lax.axis_index("mp")
    z, y = lax.div(dp, 2), lax.rem(dp, 2)
    x, core = lax.div(mp, 2), lax.rem(mp, 2)
    C = len(ff_cuts)

    def zdev(d):
        return (lax.rem(z + d, Z) * 2 + y, mp)

    def xdev(d):
        return (dp, lax.rem(x + d, R) * 2 + core)

    ydev = (z * 2 + 1 - y, mp)
    sib = (dp, x * 2 + 1 - core)

    tok, H = s["tok"], Z // 2
    h0, z2 = lax.rem(z + y, 2), lax.div(z, 2)

    def at_distance(h, i, across):
        yy = 1 - y if across else y
        k = 2 * i + lax.rem(yy + h, 2)
        return k, lax.rem(z + Z - k, Z)

    own = pltpu.make_async_copy(tok_hbm, tok.at[h0, z2, y], s["own_sem"])
    own.start()
    loads = []
    for c, (at, n) in enumerate(ff_cuts):
        pair = [
            pltpu.make_async_copy(w.at[:, pl.ds(at, n)], s["wgu"][c].at[g], s["w_sem"].at[g, c])
            for g, w in enumerate((gate_hbm, up_hbm))
        ]
        for p in pair:
            p.start()
        loads.append(pair)
    downs = []
    for c, (at, n) in enumerate(ff_cuts):
        p = pltpu.make_async_copy(down_hbm.at[pl.ds(at, n)], s["wd"][c], s["w_sem"].at[2, c])
        p.start()
        downs.append(p)

    barrier = pltpu.get_barrier_semaphore()
    peers = [ydev, sib] + [zdev(d) for d in range(1, Z)] + [xdev(d) for d in range(1, R)]
    for peer in peers:
        pl.semaphore_signal(barrier, inc=1, device_id=peer, device_id_type=MESH)
    pl.semaphore_wait(barrier, len(peers))

    copies = Copies()

    mine = tok.at[h0, z2, y]
    first = [
        copies.make(tok_hbm, mine, s["tz_sem"].at[0, d], s["tz_sem"].at[1, d], zdev(d))
        for d in range(1, Z)
    ]
    first.append(
        copies.make(tok_hbm, mine, s["ty_sem"].at[0, 0], s["ty_sem"].at[1, 0], ydev)
    )

    def send_own(h):
        @pl.when(h0 == h)
        def _():
            for copy in first:
                copy.start()

    def pass_on(h):
        for i in range(H):
            _, d = at_distance(h, i, False)

            @pl.when(d > 0)
            def _():
                block = tok.at[h, i, y]
                arrived(block, s["tz_sem"].at[0, d], s["tz_sem"].at[1, d], zdev(1))
                pltpu.make_async_remote_copy(
                    src_ref=block, dst_ref=block, send_sem=s["ty_sem"].at[0, d],
                    recv_sem=s["ty_sem"].at[1, d], device_id=ydev, device_id_type=MESH,
                ).start()

    def gathered(h):
        for i in range(H):
            _, d = at_distance(h, i, True)
            arrived(
                tok.at[h, i, 1 - y], s["ty_sem"].at[0, d], s["ty_sem"].at[1, d], ydev
            )

    rows = tok.shape[1] * 2 * tok.shape[3]
    width = tok.shape[4]
    q = rows // (2 * R)

    def project(h, c):
        n = ff_cuts[c][1]
        count, step = tiles(n)
        part, w = s["part"][h][c], s["wgu"][c]
        if h == 0:
            for g in range(2):
                loads[c][g].wait()

        def body(j, _):
            cols = pl.ds(pl.multiple_of(j * step, 128), step) if count > 1 else slice(None)
            for g in range(2):
                p = jnp.dot(
                    tok[h].reshape(rows, width), w[g, :, cols], preferred_element_type=F32
                ).reshape(R, 2, q, step)
                for k in range(2):
                    part[k, g, :, :, cols] = p[:, k]
            return 0

        if count > 1:
            lax.fori_loop(0, count, body, 0)
        else:
            body(0, 0)
        copies.start(
            part.at[1 - core], s["rx1"][h][c], s["s1_sem"].at[0, h, c], s["s1_sem"].at[1, h, c], sib
        )

    def share(h, c):
        part, rx1 = s["part"][h][c], s["rx1"][h][c]
        arrived(rx1, s["s1_sem"].at[0, h, c], s["s1_sem"].at[1, h, c], sib)
        for d in range(1, R):
            r = lax.rem(x + d, R)
            for g in range(2):
                s["tx2"][h][c][d - 1, g] = (part[core, g, r] + rx1[g, r]).astype(BF16)
            copies.start(
                s["tx2"][h][c].at[d - 1], s["rx2"][h][c].at[d - 1],
                s["s2_sem"].at[0, h, c, d], s["s2_sem"].at[1, h, c, d], xdev(d),
            )

    def activate(h, c):
        part, rx1, rx2, hid = s["part"][h][c], s["rx1"][h][c], s["rx2"][h][c], s["hid"][h][c]
        for d in range(1, R):
            arrived(rx2.at[d - 1], s["s2_sem"].at[0, h, c, d], s["s2_sem"].at[1, h, c, d], xdev(d))
        sums = []
        for g in range(2):
            v = part[core, g, x] + rx1[g, x]
            for d in range(1, R):
                v = v + rx2[d - 1, g].astype(F32)
            sums.append(v)
        gate, up = sums
        hid[x, core] = (gate / (1.0 + jnp.exp(-gate)) * up).astype(BF16)
        block = hid.at[x, core]
        for d in range(1, R):
            copies.start(
                block, block, s["s3_sem"].at[0, h, c, d], s["s3_sem"].at[1, h, c, d], xdev(d)
            )
        copies.start(block, block, s["s4_sem"].at[0, h, c, 0], s["s4_sem"].at[1, h, c, 0], sib)

    def forward(h, c):
        hid = s["hid"][h][c]
        for d in range(1, R):
            block = hid.at[lax.rem(x + R - d, R), core]
            arrived(block, s["s3_sem"].at[0, h, c, d], s["s3_sem"].at[1, h, c, d], xdev(d))
            copies.start(block, block, s["s4_sem"].at[0, h, c, d], s["s4_sem"].at[1, h, c, d], sib)

    acc = s["acc"]

    def mix(h, c, first, last):
        n = ff_cuts[c][1]
        hid, wd = s["hid"][h][c], s["wd"][c]
        for d in range(R):
            block = hid.at[lax.rem(x + R - d, R), 1 - core]
            arrived(block, s["s4_sem"].at[0, h, c, d], s["s4_sem"].at[1, h, c, d], sib)
        if h == 0:
            downs[c].wait()
        for j, (at, m) in enumerate(out_cuts):
            count, step = tiles(m)

            def body(i, _):
                cols = pl.ds(pl.multiple_of(at + i * step, 128), step)
                p = jnp.dot(
                    hid[...].reshape(rows, n), wd[:, cols], preferred_element_type=F32
                ).reshape(H, 2, rows // Z, step)
                if not first:
                    p = p + acc[h, :, :, :, cols]
                acc[h, :, :, :, cols] = p
                return 0

            lax.fori_loop(0, count, body, 0)
            if last:
                ysend(h, j)

    def ysend(h, j):
        at, m = out_cuts[j]
        ty, ry = s["ty"][j].at[h], s["ry"][j].at[h]
        for i in range(H):
            ty[i] = acc[h, i, 1 - y, :, at:at + m].astype(BF16)
        copies.start(ty, ry, s["y_sem"].at[0, h, j], s["y_sem"].at[1, h, j], ydev)

    def zsend(h, j):
        at, m = out_cuts[j]
        ry, tz, rz = s["ry"][j].at[h], s["tz"][j], s["rz"][j]
        arrived(ry, s["y_sem"].at[0, h, j], s["y_sem"].at[1, h, j], ydev)
        for i in range(H):
            k = 2 * i + lax.rem(y + h, 2)
            d = lax.rem(k + Z - z, Z)

            @pl.when(d > 0)
            def _():
                tz[d - 1] = (acc[h, i, y, :, at:at + m] + ry[i].astype(F32)).astype(BF16)
                pltpu.make_async_remote_copy(
                    src_ref=tz.at[d - 1], dst_ref=rz.at[d - 1],
                    send_sem=s["z_sem"].at[0, j, d], recv_sem=s["z_sem"].at[1, j, d],
                    device_id=zdev(d), device_id_type=MESH,
                ).start()

    def finish(j):
        at, m = out_cuts[j]
        rz = s["rz"][j]
        v = acc[h0, z2, y, :, at:at + m] + s["ry"][j][h0, z2].astype(F32)
        for d in range(1, Z):
            arrived(rz.at[d - 1], s["z_sem"].at[0, j, d], s["z_sem"].at[1, j, d], zdev(d))
            v = v + rz[d - 1].astype(F32)
        out_ref[:, at:at + m] = v.astype(BF16)

    J = len(out_cuts)
    send_own(0)
    send_own(1)
    pass_on(0)
    pass_on(1)
    own.wait()
    gathered(0)
    for c in range(C):
        project(0, c)
        if c:
            share(0, c - 1)
    share(0, C - 1)
    gathered(1)
    for c in range(C):
        project(1, c)
        if c:
            share(1, c - 1)
        activate(0, c)
    share(1, C - 1)
    for c in range(C):
        forward(0, c)
    for c in range(C):
        mix(0, c, c == 0, c == C - 1)
        activate(1, c)
    for c in range(C):
        forward(1, c)
        if c:
            mix(1, c - 1, c == 1, False)
    for j in range(J):
        zsend(0, j)
    mix(1, C - 1, C == 1, True)
    for j in range(J):
        zsend(1, j)
    for j in range(J):
        finish(j)
    for copy in copies.sent:
        copy.wait_send()
    for d in range(1, Z):
        pltpu.make_async_remote_copy(
            src_ref=mine, dst_ref=mine, send_sem=s["ty_sem"].at[0, d],
            recv_sem=s["ty_sem"].at[1, d], device_id=ydev, device_id_type=MESH,
        ).wait_send()
        for j in range(J):
            block = s["tz"][j].at[d - 1]
            pltpu.make_async_remote_copy(
                src_ref=block, dst_ref=block, send_sem=s["z_sem"].at[0, j, d],
                recv_sem=s["z_sem"].at[1, j, d], device_id=zdev(d), device_id_type=MESH,
            ).wait_send()


def shards(ndp, nmp, tokens, gate_weight, up_weight, down_weight):
    Z, R = ndp // 2, nmp // 2
    t, width = tokens.shape
    hidden, features = down_weight.shape
    ff_cuts, out_cuts = cuts(hidden, 768), cuts(features, 512)
    C, J = len(ff_cuts), len(out_cuts)
    H, q = Z // 2, t * ndp // (2 * nmp)
    dma = pltpu.SemaphoreType.DMA
    V = pltpu.VMEM
    scratch = {
        "tok": V((2, H, 2, t, width), BF16),
        "wgu": [V((2, width, n), BF16) for _, n in ff_cuts],
        "wd": [V((n, features), BF16) for _, n in ff_cuts],
        "part": [[V((2, 2, R, q, n), F32) for _, n in ff_cuts] for _ in range(2)],
        "rx1": [[V((2, R, q, n), F32) for _, n in ff_cuts] for _ in range(2)],
        "tx2": [[V((R - 1, 2, q, n), BF16) for _, n in ff_cuts] for _ in range(2)],
        "rx2": [[V((R - 1, 2, q, n), BF16) for _, n in ff_cuts] for _ in range(2)],
        "hid": [[V((R, 2, q, n), BF16) for _, n in ff_cuts] for _ in range(2)],
        "acc": V((2, H, 2, t, features), F32),
        "ty": [V((2, H, t, m), BF16) for _, m in out_cuts],
        "ry": [V((2, H, t, m), BF16) for _, m in out_cuts],
        "tz": [V((Z - 1, t, m), BF16) for _, m in out_cuts],
        "rz": [V((Z - 1, t, m), BF16) for _, m in out_cuts],
        "own_sem": dma,
        "w_sem": dma((3, C)),
        "tz_sem": dma((2, Z)),
        "ty_sem": dma((2, Z)),
        "s1_sem": dma((2, 2, C)),
        "s2_sem": dma((2, 2, C, R)),
        "s3_sem": dma((2, 2, C, R)),
        "s4_sem": dma((2, 2, C, R)),
        "y_sem": dma((2, 2, J)),
        "z_sem": dma((2, J, Z)),
    }
    leaves, tree = jax.tree.flatten(scratch)

    def body(*refs):
        kernel(Z, R, ff_cuts, out_cuts, *refs[:5], jax.tree.unflatten(tree, refs[5:]))

    flops = 6 * t * ndp * width * hidden
    return pl.pallas_call(
        body,
        out_shape=jax.ShapeDtypeStruct((t, features), BF16),
        in_specs=[pl.BlockSpec(memory_space=pl.ANY)] * 4,
        out_specs=pl.BlockSpec(memory_space=pltpu.VMEM),
        scratch_shapes=leaves,
        compiler_params=pltpu.CompilerParams(
            collective_id=0, has_side_effects=True, vmem_limit_bytes=58 * 2**20
        ),
        cost_estimate=pl.CostEstimate(
            flops=flops, bytes_accessed=6 * width * hidden, transcendentals=0
        ),
        name="ffn",
    )(tokens, gate_weight, up_weight, down_weight)


def solution(mesh):
    return jax.shard_map(
        functools.partial(shards, mesh.shape["dp"], mesh.shape["mp"]),
        mesh=mesh,
        in_specs=(P("dp", "mp"), P("mp", "dp"), P("mp", "dp"), P("dp", "mp")),
        out_specs=P("dp", "mp"),
        check_vma=False,
    )
```
